1024 devices in a mesh: blk: 32 (over x, y_hi), grp: 32 (over z, y_lo, core).
Axes of the slice: x: 8, y: 8 (y_hi: 4, y_lo: 2; y = y_hi * 2 + y_lo), z: 8, core: 2. Of those that a mesh axis runs over, the one named last changes fastest.
Arguments:
- image: bfloat16 [262144, 1152], P(('blk', 'grp')), may hold values from -0.1875 to 0.1875
- text: bfloat16 [262144, 1152], P(('blk', 'grp')), may hold values from -0.1875 to 0.1875
- log_temp: float32 [1], replicated, may hold values from 1.6 to 3
- bias: float32 [1], replicated, may hold values from -4 to -1
Outputs:
- grad_image: float32 [262144, 1152], P(('blk', 'grp'))
- grad_text: float32 [262144, 1152], P(('blk', 'grp'))
- grad_log_temp: float32 [1], replicated
- grad_bias: float32 [1], replicated
The draws below stay inside these ranges and needn't reach their ends.
All inputs are finite; a program needn't handle non-finite values.
Results may differ from the reference program's by a relative error of at most 0.0024.
Values may be sent and summed in bfloat16 or wider, within the bound.
A program may use at most 32 MiB of HBM per device.

```python
import jax
import jax.numpy as jnp
from jax import lax

D = 1152
TOK_DEV = 256
TOKENS = 262144
SHIFT = 8192
N_BLK = 32
N_GRP = 32


cluster_count = 16


edge_value = 0.1875


def shared_parts(key):
    keys = jax.random.split(key, 6)
    centers = jax.random.normal(keys[0], (cluster_count, D), jnp.float32)
    assign = jax.random.randint(keys[1], (TOKENS,), 0, cluster_count)
    place = jnp.arange(TOKENS, dtype=jnp.int32) // SHIFT
    strength = jax.random.uniform(keys[2], (N_BLK,), jnp.float32, 0.25, 0.7)[place][:, None]
    paired = jax.random.uniform(keys[3], (N_BLK,), jnp.float32, 0.2, 0.9)[place][:, None]
    first = jax.random.normal(keys[4], (TOKENS, D), jnp.float32)
    second = jax.random.normal(keys[5], (TOKENS, D), jnp.float32)
    return (centers[assign] * strength, strength, paired, first, second)


def finish(values, strength):
    scaled = values / jnp.sqrt(1.0 + strength * strength) * D ** (-0.5)
    return jnp.clip(scaled, -edge_value, edge_value)


def draw_image(key, part):
    common, strength, paired, first, second = shared_parts(key)
    values = common + first
    return finish(values, strength).astype(jnp.bfloat16)


def draw_text(key, part):
    common, strength, paired, first, second = shared_parts(key)
    rest = jnp.sqrt(1.0 - paired * paired)
    values = common + paired * first + rest * second
    return finish(values, strength).astype(jnp.bfloat16)


def setup_inputs(seed: int = 0) -> dict:
    splits = jax.random.split(jax.random.key(seed), 5)
    return {
        "image": draw_image(jax.random.fold_in(splits[4], 71), 0),
        "text": draw_text(jax.random.fold_in(splits[4], 71), 0),
        "log_temp": jnp.clip(jax.random.uniform(splits[2], (1,), jnp.float32, 1.6, 3.0), 1.6, 3.0),
        "bias": jnp.clip(jax.random.uniform(splits[3], (1,), jnp.float32, -4.0, -1.0), -4.0, -1.0),
    }


def unit_rows(rows_in):
    values = rows_in.astype(jnp.float32)
    length = jnp.sqrt(lax.optimization_barrier(jnp.sum(values * values, axis=-1, keepdims=True)) + 1e-06)
    return (values / length, length)

def norm_back(unit, length, grad_unit):
    inner = lax.optimization_barrier(jnp.sum(unit * grad_unit, axis=-1, keepdims=True))
    return (grad_unit - unit * inner) / length

def reference(image, text, log_temp, bias):
    temp = jnp.exp(log_temp[0])
    shift_b = bias[0]
    blocks = TOKENS // TOK_DEV
    img_blocks = image.reshape(blocks, TOK_DEV, D)
    txt_blocks = text.reshape(blocks, TOK_DEV, D)
    prev_blocks = jnp.roll(txt_blocks, N_GRP, axis=0)
    rows = lax.broadcasted_iota(jnp.int32, (TOK_DEV, TOK_DEV), 0)
    cols = lax.broadcasted_iota(jnp.int32, (TOK_DEV, TOK_DEV), 1)
    sign = jnp.where(rows == cols, 1.0, -1.0).astype(jnp.float32)

    def one_block(triple):
        img_b, txt_b, prev_b = triple
        img_unit, img_len = unit_rows(img_b)
        img_half = img_unit.astype(jnp.bfloat16)
        txt_half = unit_rows(txt_b)[0].astype(jnp.bfloat16)
        prev_half = unit_rows(prev_b)[0].astype(jnp.bfloat16)
        own = temp * jnp.dot(img_half, txt_half.T, preferred_element_type=jnp.float32) + shift_b
        near = temp * jnp.dot(img_half, prev_half.T, preferred_element_type=jnp.float32) + shift_b
        coef_own = -sign * jax.nn.sigmoid(-sign * own)
        coef_near = jax.nn.sigmoid(near)
        half_own = coef_own.astype(jnp.bfloat16)
        half_near = coef_near.astype(jnp.bfloat16)
        d_img = temp * (jnp.dot(half_own, txt_half, preferred_element_type=jnp.float32) + jnp.dot(half_near, prev_half, preferred_element_type=jnp.float32))
        grad_img = norm_back(img_unit, img_len, d_img)
        own_txt = temp * jnp.dot(half_own.T, img_half, preferred_element_type=jnp.float32)
        outgoing = temp * jnp.dot(half_near.T, img_half, preferred_element_type=jnp.float32)
        sum_c = jnp.sum(coef_own) + jnp.sum(coef_near)
        sum_cl = jnp.sum(coef_own * (own - shift_b)) + jnp.sum(coef_near * (near - shift_b))
        return (grad_img, own_txt, outgoing, sum_c, sum_cl)
    grad_img, own_txt, outgoing, sum_c, sum_cl = lax.map(one_block, (img_blocks, txt_blocks, prev_blocks))
    d_txt = own_txt + jnp.roll(outgoing, -N_GRP, axis=0)

    def text_back(pair):
        txt_b, d_b = pair
        txt_unit, txt_len = unit_rows(txt_b)
        return norm_back(txt_unit, txt_len, d_b)
    grad_txt = lax.map(text_back, (txt_blocks, d_txt))
    scale = jnp.float32(TOKENS)
    return (grad_img.reshape(TOKENS, D), grad_txt.reshape(TOKENS, D), (jnp.sum(sum_cl) / scale).reshape(1), (jnp.sum(sum_c) / scale).reshape(1))
```

```python
import functools

import jax
import jax.numpy as jnp
from jax import lax
from jax.experimental import pallas as pl
from jax.experimental.pallas import tpu as pltpu
from jax.sharding import PartitionSpec as P

MESH = pl.DeviceIdType.MESH
Y_HI, Y_LO, CORES = 4, 2, 2
CHUNKS = 8
HOLD = 5


def row_dot(left, right):
    return lax.dot_general(
        left, right, (((1,), (1,)), ((), ())), preferred_element_type=jnp.float32
    )


def plain_dot(left, right):
    return lax.dot_general(
        left, right, (((1,), (0,)), ((), ())), preferred_element_type=jnp.float32
    )


def fold(tile):
    rows, cols = tile.shape
    part = jnp.sum(tile.reshape(rows // 8, 8, cols), axis=0)
    return functools.reduce(
        jnp.add, [part[:, at : at + 128] for at in range(0, cols, 128)]
    )


def kernel(
    sizes, img_in, txt_in, log_temp, bias, gi_out, gt_out, cl_out, c_out,
    img_raw, txt_raw, img_half, txt_half, img_inv, txt_inv,
    mid_txt, mid_img, end_txt, end_img, acc_txt, acc_img, sums,
    part, load_sem, send_sem, recv_sem, sum_send, sum_recv,
):
    blk_n, grp_n, total_pairs = sizes
    x_n, z_n = blk_n // Y_HI, grp_n // (Y_LO * CORES)
    rows = img_raw.shape[0]
    step = rows // CHUNKS

    me, grp = lax.axis_index("blk"), lax.axis_index("grp")
    x, y_hi = lax.div(me, Y_HI), lax.rem(me, Y_HI)
    z, low = lax.div(grp, Y_LO * CORES), lax.rem(grp, Y_LO * CORES)
    y_lo, core = lax.div(low, CORES), lax.rem(low, CORES)
    y = y_hi * Y_LO + y_lo

    def at(x, y, z, core):
        return (
            x * Y_HI + lax.div(y, Y_LO),
            z * (Y_LO * CORES) + lax.rem(y, Y_LO) * CORES + core,
        )

    other = z * (Y_LO * CORES) + (1 - y_lo) * CORES + core
    before = lax.rem(me + blk_n - 1, blk_n)
    meet_next = (x * Y_HI + lax.rem(y_hi + y_lo, Y_HI), other)
    meet_prev = (
        lax.div(before, Y_HI) * Y_HI + lax.rem(lax.rem(before, Y_HI) + y_lo, Y_HI),
        other,
    )
    first_blk = x * Y_HI + lax.rem(y_hi + y_lo + Y_HI - 1, Y_HI)
    first = (first_blk, other)
    second = (lax.rem(first_blk + 1, blk_n), other)

    levels = (
        (CORES, core, lambda k: at(x, y, z, k)),
        (z_n, z, lambda k: at(x, y, k, core)),
        (x_n, x, lambda k: at(k, y, z, core)),
        (Y_HI * Y_LO, y, lambda k: at(x, k, z, core)),
    )

    loads = [
        pltpu.make_async_copy(img_in, img_raw, load_sem.at[0]),
        pltpu.make_async_copy(txt_in, txt_raw, load_sem.at[1]),
    ]
    for load in loads:
        load.start()

    barrier = pltpu.get_barrier_semaphore()
    greeted = 0
    for device in (meet_next, meet_prev, first, second):
        pl.semaphore_signal(barrier, inc=1, device_id=device, device_id_type=MESH)
        greeted += 1
    for count, mine, place in levels:
        for k in range(1, count):
            pl.semaphore_signal(
                barrier, inc=1, device_id=place(lax.rem(mine + k, count)),
                device_id_type=MESH,
            )
            greeted += 1

    temp = jnp.exp(jnp.full((1, 1), log_temp[0], jnp.float32))
    shift = bias[0]

    def window(c):
        return pl.ds(c * step, step)

    def remote(src, dst, kind, c, device):
        return pltpu.make_async_remote_copy(
            src_ref=src.at[window(c), :],
            dst_ref=dst.at[window(c), :],
            send_sem=send_sem.at[kind, c],
            recv_sem=recv_sem.at[kind, c],
            device_id=device,
            device_id_type=MESH,
        )

    def normalize(raw, half, inv, c):
        values = raw[window(c), :].astype(jnp.float32)
        scale = 1.0 / jnp.sqrt(jnp.sum(values * values, axis=-1, keepdims=True) + 1e-06)
        inv[window(c), :] = scale
        half[window(c), :] = (values * scale).astype(jnp.bfloat16)

    for load in loads:
        load.wait()
    for c in range(CHUNKS):
        normalize(txt_raw, txt_half, txt_inv, c)
        normalize(img_raw, img_half, img_inv, c)
        if c == 0:
            pl.semaphore_wait(barrier, greeted)
        remote(txt_half, mid_txt, 0, c, meet_next).start()
        remote(img_half, mid_img, 1, c, meet_prev).start()

    def coefs(sims, diagonal):
        scaled = temp * sims
        logit = scaled + shift
        if not diagonal:
            return jax.nn.sigmoid(logit), scaled
        row = lax.broadcasted_iota(jnp.int32, sims.shape, 0)
        col = lax.broadcasted_iota(jnp.int32, sims.shape, 1)
        paired = row == col
        coef = jax.nn.sigmoid(jnp.where(paired, -logit, logit))
        return jnp.where(paired, -coef, coef), scaled

    coef, scaled = coefs(row_dot(img_half[...], txt_half[...]), True)
    own_c, own_cl = fold(coef), fold(coef * scaled)
    half = coef.astype(jnp.bfloat16)
    acc_img[...] = plain_dot(half, txt_half[...])
    half = coef.T.astype(jnp.bfloat16)
    acc_txt[...] = plain_dot(half, img_half[...])

    def arrived(c):
        remote(txt_half, mid_txt, 0, c, meet_next).wait_recv()
        remote(img_half, mid_img, 1, c, meet_prev).wait_recv()

    def send_on(c):
        remote(mid_txt, end_txt, 2, c, second).start()
        remote(mid_img, end_img, 3, c, first).start()

    for c in range(HOLD):
        arrived(c)
    for c in range(HOLD):
        send_on(c)
    for c in range(HOLD, CHUNKS):
        arrived(c)
        send_on(c)

    coef, scaled = coefs(row_dot(mid_img[...], mid_txt[...]), False)
    part[0:8, :] = own_c + fold(coef)
    part[8:16, :] = own_cl + fold(coef * scaled)
    tile = jnp.concatenate(
        [
            jnp.sum(part[0:8, :], axis=0, keepdims=True),
            jnp.sum(part[8:16, :], axis=0, keepdims=True),
            jnp.zeros((6, 128), jnp.float32),
        ],
        axis=0,
    )

    def exchange(level, mine, place, k, count):
        return pltpu.make_async_remote_copy(
            src_ref=sums.at[level, mine],
            dst_ref=sums.at[level, mine],
            send_sem=sum_send.at[level, k],
            recv_sem=sum_recv.at[level, mine],
            device_id=place(lax.rem(mine + k, count)),
            device_id_type=MESH,
        )

    for level, (count, mine, place) in enumerate(levels):
        sums[level, mine] = tile
        for k in range(1, count):
            exchange(level, mine, place, k, count).start()
        for k in range(1, count):
            source = lax.rem(mine + k, count)
            pltpu.make_async_remote_copy(
                src_ref=sums.at[level, source],
                dst_ref=sums.at[level, source],
                send_sem=sum_send.at[level, k],
                recv_sem=sum_recv.at[level, source],
                device_id=place(source),
                device_id_type=MESH,
            ).wait_recv()
        tile = sums[level, 0]
        for k in range(1, count):
            tile = tile + sums[level, k]
    c_out[0] = jnp.sum(tile[0:1, :]) / total_pairs
    cl_out[0] = jnp.sum(tile[1:2, :]) / total_pairs

    def finish(raw, half, inv, acc, visitors, out):
        coef, _ = coefs(row_dot(half[...], visitors[...]), False)
        grad = temp * (acc[...] + plain_dot(coef.astype(jnp.bfloat16), visitors[...]))
        scale = inv[...]
        unit = raw[...].astype(jnp.float32) * scale
        inner = jnp.sum(unit * grad, axis=-1, keepdims=True)
        out[...] = (grad - unit * inner) * scale

    for c in range(CHUNKS):
        remote(mid_txt, end_txt, 2, c, second).wait_recv()
    finish(img_raw, img_half, img_inv, acc_img, end_txt, gi_out)
    for c in range(CHUNKS):
        remote(mid_img, end_img, 3, c, first).wait_recv()
    finish(txt_raw, txt_half, txt_inv, acc_txt, end_img, gt_out)

    for c in range(CHUNKS):
        remote(txt_half, mid_txt, 0, c, meet_next).wait_send()
        remote(img_half, mid_img, 1, c, meet_prev).wait_send()
        remote(mid_txt, end_txt, 2, c, second).wait_send()
        remote(mid_img, end_img, 3, c, first).wait_send()
    for level, (count, mine, place) in enumerate(levels):
        for k in range(1, count):
            exchange(level, mine, place, k, count).wait_send()


def local(blk_n, grp_n, image, text, log_temp, bias):
    rows, width = image.shape
    most = max(CORES, grp_n // (Y_LO * CORES), blk_n // Y_HI, Y_HI * Y_LO)
    wide = jax.ShapeDtypeStruct((rows, width), jnp.float32)
    one = jax.ShapeDtypeStruct((1,), jnp.float32)
    half = pltpu.VMEM((rows, width), jnp.bfloat16)
    full = pltpu.VMEM((rows, width), jnp.float32)
    thin = pltpu.VMEM((rows, 1), jnp.float32)
    vmem, smem = pl.BlockSpec(memory_space=pltpu.VMEM), pl.BlockSpec(memory_space=pltpu.SMEM)
    hbm = pl.BlockSpec(memory_space=pl.ANY)
    dma = pltpu.SemaphoreType.DMA
    grad_image, grad_text, total_cl, total_c = pl.pallas_call(
        functools.partial(kernel, (blk_n, grp_n, float(rows * blk_n * grp_n))),
        out_shape=(wide, wide, one, one),
        in_specs=[hbm, hbm, smem, smem],
        out_specs=(vmem, vmem, smem, smem),
        scratch_shapes=[
            half, half, half, half, thin, thin,
            half, half, half, half, full, full,
            pltpu.VMEM((4, most, 8, 128), jnp.float32),
            pltpu.VMEM((16, 128), jnp.float32),
            dma((2,)), dma((4, CHUNKS)), dma((4, CHUNKS)),
            dma((4, most)), dma((4, most)),
        ],
        compiler_params=pltpu.CompilerParams(
            collective_id=0, has_side_effects=True, vmem_limit_bytes=40 << 20
        ),
        name="pair_gradients",
    )(image, text, log_temp, bias)
    return grad_image, grad_text, total_cl, total_c


def solution(mesh):
    rows = P(("blk", "grp"), None)
    return jax.shard_map(
        functools.partial(local, mesh.shape["blk"], mesh.shape["grp"]),
        mesh=mesh,
        in_specs=(rows, rows, P(), P()),
        out_specs=(rows, rows, P(), P()),
        check_vma=False,
    )
```

```python
import functools

import jax
import jax.numpy as jnp
from jax import lax
from jax.experimental import pallas as pl
from jax.experimental.pallas import tpu as pltpu
from jax.sharding import PartitionSpec as P

MESH = pl.DeviceIdType.MESH
Y_HI, Y_LO, CORES = 4, 2, 2
CHUNKS = 8
PARTS = 4
TURNS = 3


def row_dot(left, right):
    return lax.dot_general(
        left, right, (((1,), (1,)), ((), ())), preferred_element_type=jnp.float32
    )


def plain_dot(left, right):
    return lax.dot_general(
        left, right, (((1,), (0,)), ((), ())), preferred_element_type=jnp.float32
    )


def fold(tile):
    rows, cols = tile.shape
    part = jnp.sum(tile.reshape(rows // 8, 8, cols), axis=0)
    return functools.reduce(
        jnp.add, [part[:, at : at + 128] for at in range(0, cols, 128)]
    )


def kernel(
    sizes, img_in, txt_in, log_temp, bias, gi_out, gt_out, sum_out,
    img_raw, txt_raw, img_half, txt_half, img_inv, txt_inv,
    mid_txt, mid_img, end_txt, end_img, acc_txt, acc_img, sums,
    part, climb, total, load_sem, send_sem, recv_sem, sum_send, sum_recv, climb_sem, drop_sem,
    here_sem, base_sem, round_sem,
):
    blk_n, grp_n = sizes
    x_n, z_n = blk_n // Y_HI, grp_n // (Y_LO * CORES)
    rows = img_raw.shape[0]
    step = rows // CHUNKS

    me, grp = lax.axis_index("blk"), lax.axis_index("grp")
    x, y_hi = lax.div(me, Y_HI), lax.rem(me, Y_HI)
    z, low = lax.div(grp, Y_LO * CORES), lax.rem(grp, Y_LO * CORES)
    y_lo, core = lax.div(low, CORES), lax.rem(low, CORES)
    y = y_hi * Y_LO + y_lo

    def at(x, y, z, core):
        return (
            x * Y_HI + lax.div(y, Y_LO),
            z * (Y_LO * CORES) + lax.rem(y, Y_LO) * CORES + core,
        )

    other = z * (Y_LO * CORES) + (1 - y_lo) * CORES + core
    before = lax.rem(me + blk_n - 1, blk_n)
    meet_next = (x * Y_HI + lax.rem(y_hi + y_lo, Y_HI), other)
    meet_prev = (
        lax.div(before, Y_HI) * Y_HI + lax.rem(lax.rem(before, Y_HI) + y_lo, Y_HI),
        other,
    )
    first_blk = x * Y_HI + lax.rem(y_hi + y_lo + Y_HI - 1, Y_HI)
    first = (first_blk, other)
    second = (lax.rem(first_blk + 1, blk_n), other)

    base = z == 0

    def along(k):
        return at(x, lax.rem(y + k, Y_HI * Y_LO), z, core)

    def across(k):
        return at(lax.rem(x + k, x_n), y, z, core)

    def twin(k):
        return at(x, y, z, lax.rem(core + k, CORES))

    levels = (
        (Y_HI * Y_LO, y, along),
        (CORES, core, twin),
        (x_n, x, across),
    )

    loads = [
        pltpu.make_async_copy(img_in, img_raw, load_sem.at[0]),
        pltpu.make_async_copy(txt_in, txt_raw, load_sem.at[1]),
    ]
    for load in loads:
        load.start()

    barrier = pltpu.get_barrier_semaphore()

    def greet(device):
        pl.semaphore_signal(barrier, inc=1, device_id=device, device_id_type=MESH)

    for device in (meet_next, meet_prev, first, second):
        greet(device)

    @pl.when(z < z_n - 1)
    def _():
        greet(at(x, y, z + 1, core))

    beside = (across(1), across(x_n - 1), along(1), along(Y_HI * Y_LO - 1))

    @pl.when(base)
    def _():
        greet(beside[0])
        greet(beside[1])
        for k in range(1, CORES):
            greet(twin(k))

    greeted = 4 + (z > 0).astype(jnp.int32) + base.astype(jnp.int32) * (1 + CORES)

    def signal(sem, device):
        pl.semaphore_signal(sem, inc=1, device_id=device, device_id_type=MESH)

    def tell(turn):
        for device in beside:
            signal(round_sem.at[turn], device)

    temp = jnp.exp(jnp.full((1, 1), log_temp[0], jnp.float32))
    shift = bias[0]

    def window(c):
        return pl.ds(c * step, step)

    def remote(src, dst, kind, c, device):
        return pltpu.make_async_remote_copy(
            src_ref=src.at[window(c), :],
            dst_ref=dst.at[window(c), :],
            send_sem=send_sem.at[kind, c],
            recv_sem=recv_sem.at[kind, c],
            device_id=device,
            device_id_type=MESH,
        )

    def normalize(raw, half, inv, c):
        values = raw[window(c), :].astype(jnp.float32)
        scale = 1.0 / jnp.sqrt(jnp.sum(values * values, axis=-1, keepdims=True) + 1e-06)
        inv[window(c), :] = scale
        half[window(c), :] = (values * scale).astype(jnp.bfloat16)

    for load in loads:
        load.wait()
    for c in range(CHUNKS):
        normalize(txt_raw, txt_half, txt_inv, c)
        normalize(img_raw, img_half, img_inv, c)
        if c == 0:
            pl.semaphore_wait(barrier, greeted)
        remote(txt_half, mid_txt, 0, c, meet_next).start()
        remote(img_half, mid_img, 1, c, meet_prev).start()

    @pl.when(z > 1)
    def _():
        signal(here_sem, at(x, y, z - 1, core))

    @pl.when(base)
    def _():
        tell(0)

    def coefs(sims, diagonal):
        scaled = temp * sims
        logit = scaled + shift
        if not diagonal:
            return jax.nn.sigmoid(logit), scaled
        row = lax.broadcasted_iota(jnp.int32, sims.shape, 0)
        col = lax.broadcasted_iota(jnp.int32, sims.shape, 1)
        paired = row == col
        coef = jax.nn.sigmoid(jnp.where(paired, -logit, logit))
        return jnp.where(paired, -coef, coef), scaled

    coef, scaled = coefs(row_dot(img_half[...], txt_half[...]), True)
    own_c, own_cl = fold(coef), fold(coef * scaled)
    half = coef.astype(jnp.bfloat16)
    acc_img[...] = plain_dot(half, txt_half[...])
    half = coef.T.astype(jnp.bfloat16)
    acc_txt[...] = plain_dot(half, img_half[...])

    @pl.when(z > 1)
    def _():
        pl.semaphore_wait(base_sem, 1)

    @pl.when(jnp.logical_and(z > 0, z < z_n - 1))
    def _():
        pl.semaphore_wait(here_sem, 1)
        signal(base_sem, at(x, y, z + 1, core))

    def arrived(c):
        remote(txt_half, mid_txt, 0, c, meet_next).wait_recv()
        remote(img_half, mid_img, 1, c, meet_prev).wait_recv()

    def send_on(c):
        remote(mid_txt, end_txt, 2, c, second).start()
        remote(mid_img, end_img, 3, c, first).start()

    for c in range(CHUNKS):
        arrived(c)

    coef, scaled = coefs(row_dot(mid_img[...], mid_txt[...]), False)
    part[0:8, :] = own_c + fold(coef)
    part[8:16, :] = own_cl + fold(coef * scaled)
    tile = jnp.concatenate(
        [
            jnp.sum(part[0:8, :], axis=0, keepdims=True),
            jnp.sum(part[8:16, :], axis=0, keepdims=True),
            jnp.zeros((6, 128), jnp.float32),
        ],
        axis=0,
    )

    climb[0] = tile

    def rise(k):
        return pltpu.make_async_remote_copy(
            src_ref=climb.at[0],
            dst_ref=climb.at[k],
            send_sem=climb_sem.at[0],
            recv_sem=climb_sem.at[k],
            device_id=at(x, y, 0, core),
            device_id_type=MESH,
        )

    def drop(k):
        return pltpu.make_async_remote_copy(
            src_ref=total,
            dst_ref=total,
            send_sem=drop_sem.at[k],
            recv_sem=drop_sem.at[0],
            device_id=at(x, y, k, core),
            device_id_type=MESH,
        )

    @pl.when(z > 0)
    def _():
        rise(z).start()
        rise(z).wait_send()

    for c in range(CHUNKS):
        send_on(c)

    @pl.when(base)
    def _():
        for turn in range(TURNS):
            pl.semaphore_wait(round_sem.at[turn], 4)
            if turn + 1 < TURNS:
                tell(turn + 1)

    def exchange(level, k):
        count, mine, place = levels[level]
        return pltpu.make_async_remote_copy(
            src_ref=sums.at[level, mine],
            dst_ref=sums.at[level, mine],
            send_sem=sum_send.at[level, k],
            recv_sem=sum_recv.at[level, mine],
            device_id=place(k),
            device_id_type=MESH,
        )

    def incoming(level, k):
        count, mine, place = levels[level]
        source = lax.rem(mine + k, count)
        return pltpu.make_async_remote_copy(
            src_ref=sums.at[level, source],
            dst_ref=sums.at[level, source],
            send_sem=sum_send.at[level, k],
            recv_sem=sum_recv.at[level, source],
            device_id=place(k),
            device_id_type=MESH,
        )

    def add_over(level, tile):
        count, mine, _ = levels[level]
        sums[level, mine] = tile
        for k in range(1, count):
            exchange(level, k).start()
        for k in range(1, count):
            incoming(level, k).wait_recv()
        tile = sums[level, 0]
        for k in range(1, count):
            tile = tile + sums[level, k]
        return tile

    def finish(raw, half, inv, acc, visitors, out):
        coef, _ = coefs(row_dot(half[...], visitors[...]), False)
        grad = temp * (acc[...] + plain_dot(coef.astype(jnp.bfloat16), visitors[...]))
        scale = inv[...]
        unit = raw[...].astype(jnp.float32) * scale
        inner = jnp.sum(unit * grad, axis=-1, keepdims=True)
        out[...] = (grad - unit * inner) * scale

    for c in range(CHUNKS):
        remote(mid_txt, end_txt, 2, c, second).wait_recv()
    finish(img_raw, img_half, img_inv, acc_img, end_txt, gi_out)
    for c in range(CHUNKS):
        remote(mid_img, end_img, 3, c, first).wait_recv()
    finish(txt_raw, txt_half, txt_inv, acc_txt, end_img, gt_out)

    @pl.when(base)
    def _():
        for k in range(1, z_n):
            rise(k).wait_recv()
        tile = climb[0]
        for k in range(1, z_n):
            tile = tile + climb[k]
        for level in range(len(levels)):
            tile = add_over(level, tile)
        total[...] = tile
        for k in range(1, z_n):
            drop(k).start()

    for c in range(CHUNKS):
        remote(txt_half, mid_txt, 0, c, meet_next).wait_send()
        remote(img_half, mid_img, 1, c, meet_prev).wait_send()
        remote(mid_txt, end_txt, 2, c, second).wait_send()
        remote(mid_img, end_img, 3, c, first).wait_send()

    @pl.when(z > 0)
    def _():
        drop(z).wait_recv()

    @pl.when(base)
    def _():
        for level, (count, _, _) in enumerate(levels):
            for k in range(1, count):
                exchange(level, k).wait_send()
        for k in range(1, z_n):
            drop(k).wait_send()

    sum_out[...] = total[...]


def leave(pairs, gi_in, gt_in, sum_in, gi_out, gt_out, cl_out, c_out, sem):
    rows = gi_in.shape[0]
    step = rows // PARTS
    copies = []
    for c in range(PARTS):
        part = pl.ds(c * step, step)
        for k, (src, dst) in enumerate(((gi_in, gi_out), (gt_in, gt_out))):
            copies.append(
                pltpu.make_async_copy(src.at[part, :], dst.at[part, :], sem.at[k, c])
            )
    for copy in copies:
        copy.start()
    c_out[0] = jnp.sum(sum_in[0:1, :]) / pairs
    cl_out[0] = jnp.sum(sum_in[1:2, :]) / pairs
    for copy in copies:
        copy.wait()


def local(blk_n, grp_n, image, text, log_temp, bias):
    rows, width = image.shape
    z_n = grp_n // (Y_LO * CORES)
    most = max(blk_n // Y_HI, Y_HI * Y_LO, CORES)
    wide = jax.ShapeDtypeStruct((rows, width), jnp.float32)
    one = jax.ShapeDtypeStruct((1,), jnp.float32)
    slab = jax.ShapeDtypeStruct((8, 128), jnp.float32)
    half = pltpu.VMEM((rows, width), jnp.bfloat16)
    full = pltpu.VMEM((rows, width), jnp.float32)
    thin = pltpu.VMEM((rows, 1), jnp.float32)
    vmem = pl.BlockSpec(memory_space=pltpu.VMEM)
    smem = pl.BlockSpec(memory_space=pltpu.SMEM)
    hbm = pl.BlockSpec(memory_space=pltpu.HBM)
    dma, plain = pltpu.SemaphoreType.DMA, pltpu.SemaphoreType.REGULAR
    grads_and_sums = pl.pallas_call(
        functools.partial(kernel, (blk_n, grp_n)),
        out_shape=(wide, wide, slab),
        in_specs=[hbm, hbm, smem, smem],
        out_specs=(vmem, vmem, vmem),
        scratch_shapes=[
            half, half, half, half, thin, thin,
            half, half, half, half, full, full,
            pltpu.VMEM((3, most, 8, 128), jnp.float32),
            pltpu.VMEM((16, 128), jnp.float32),
            pltpu.VMEM((z_n, 8, 128), jnp.float32),
            pltpu.VMEM((8, 128), jnp.float32),
            dma((2,)), dma((4, CHUNKS)), dma((4, CHUNKS)),
            dma((3, most)), dma((3, most)), dma((z_n,)), dma((z_n,)),
            plain, plain, pltpu.SemaphoreType.REGULAR((TURNS,)),
        ],
        compiler_params=pltpu.CompilerParams(
            collective_id=0, has_side_effects=True, vmem_limit_bytes=40 << 20
        ),
        name="pair_gradients",
    )(
        pltpu.with_memory_space_constraint(image, pltpu.HBM),
        pltpu.with_memory_space_constraint(text, pltpu.HBM),
        log_temp,
        bias,
    )
    return pl.pallas_call(
        functools.partial(leave, float(rows * blk_n * grp_n)),
        out_shape=(wide, wide, one, one),
        in_specs=[vmem, vmem, vmem],
        out_specs=(hbm, hbm, smem, smem),
        scratch_shapes=[dma((2, PARTS))],
        compiler_params=pltpu.CompilerParams(vmem_limit_bytes=8 << 20),
        name="leave",
    )(*grads_and_sums)


def solution(mesh):
    rows = P(("blk", "grp"), None)
    return jax.shard_map(
        functools.partial(local, mesh.shape["blk"], mesh.shape["grp"]),
        mesh=mesh,
        in_specs=(rows, rows, P(), P()),
        out_specs=(rows, rows, P(), P()),
        check_vma=False,
    )
```

```python
import functools

import jax
import jax.numpy as jnp
from jax import lax
from jax.experimental import pallas as pl
from jax.experimental.pallas import tpu as pltpu
from jax.sharding import PartitionSpec as P

MESH = pl.DeviceIdType.MESH
Y_HI, Y_LO, CORES = 4, 2, 2
CHUNKS = 8
PARTS = 4
TURNS = 3


def row_dot(left, right):
    return lax.dot_general(
        left, right, (((1,), (1,)), ((), ())), preferred_element_type=jnp.float32
    )


def plain_dot(left, right):
    return lax.dot_general(
        left, right, (((1,), (0,)), ((), ())), preferred_element_type=jnp.float32
    )


def fold(tile):
    rows, cols = tile.shape
    part = jnp.sum(tile.reshape(rows // 8, 8, cols), axis=0)
    return functools.reduce(
        jnp.add, [part[:, at : at + 128] for at in range(0, cols, 128)]
    )


def kernel(
    sizes, img_in, txt_in, log_temp, bias, gi_out, gt_out, sum_out,
    img_raw, txt_raw, img_half, txt_half, img_inv, txt_inv,
    mid_txt, mid_img, end_txt, end_img, acc_txt, acc_img, sums,
    part, climb, total, load_sem, send_sem, recv_sem, sum_send, sum_recv, rise_sem, climb_sem, drop_sem,
    here_sem, base_sem, round_sem,
):
    blk_n, grp_n = sizes
    x_n, z_n = blk_n // Y_HI, grp_n // (Y_LO * CORES)
    rows = img_raw.shape[0]
    step = rows // CHUNKS

    me, grp = lax.axis_index("blk"), lax.axis_index("grp")
    x, y_hi = lax.div(me, Y_HI), lax.rem(me, Y_HI)
    z, low = lax.div(grp, Y_LO * CORES), lax.rem(grp, Y_LO * CORES)
    y_lo, core = lax.div(low, CORES), lax.rem(low, CORES)
    y = y_hi * Y_LO + y_lo

    def at(x, y, z, core):
        return (
            x * Y_HI + lax.div(y, Y_LO),
            z * (Y_LO * CORES) + lax.rem(y, Y_LO) * CORES + core,
        )

    other = z * (Y_LO * CORES) + (1 - y_lo) * CORES + core
    before = lax.rem(me + blk_n - 1, blk_n)
    meet_next = (x * Y_HI + lax.rem(y_hi + y_lo, Y_HI), other)
    meet_prev = (
        lax.div(before, Y_HI) * Y_HI + lax.rem(lax.rem(before, Y_HI) + y_lo, Y_HI),
        other,
    )
    first_blk = x * Y_HI + lax.rem(y_hi + y_lo + Y_HI - 1, Y_HI)
    first = (first_blk, other)
    second = (lax.rem(first_blk + 1, blk_n), other)

    root = min(1, z_n - 1)
    base = z == root
    slot = z * CORES + core

    def along(k):
        return at(x, lax.rem(y + k, Y_HI * Y_LO), z, core)

    def across(k):
        return at(lax.rem(x + k, x_n), y, z, core)

    def rooted(k):
        return at(x, y, root, lax.rem(core + k, CORES))

    levels = (
        (Y_HI * Y_LO, y, along),
        (x_n, x, across),
    )

    loads = [
        pltpu.make_async_copy(img_in, img_raw, load_sem.at[0]),
        pltpu.make_async_copy(txt_in, txt_raw, load_sem.at[1]),
    ]
    for load in loads:
        load.start()

    barrier = pltpu.get_barrier_semaphore()

    def greet(device):
        pl.semaphore_signal(barrier, inc=1, device_id=device, device_id_type=MESH)

    for device in (meet_next, meet_prev, first, second):
        greet(device)

    @pl.when(jnp.logical_and(z >= root, z < z_n - 1))
    def _():
        greet(at(x, y, z + 1, core))

    beside = (across(1), across(x_n - 1), along(1), along(Y_HI * Y_LO - 1))

    @pl.when(base)
    def _():
        greet(beside[0])
        greet(beside[1])
        for k in range(1, CORES):
            greet(rooted(k))
        for k in range(root):
            greet(at(x, y, k, core))

    greeted = 4 + jnp.where(base, 1 + CORES, 1)

    def signal(sem, device):
        pl.semaphore_signal(sem, inc=1, device_id=device, device_id_type=MESH)

    def tell(turn):
        for device in beside:
            signal(round_sem.at[turn], device)

    temp = jnp.exp(jnp.full((1, 1), log_temp[0], jnp.float32))
    shift = bias[0]

    def window(c):
        return pl.ds(c * step, step)

    def remote(src, dst, kind, c, device):
        return pltpu.make_async_remote_copy(
            src_ref=src.at[window(c), :],
            dst_ref=dst.at[window(c), :],
            send_sem=send_sem.at[kind, c],
            recv_sem=recv_sem.at[kind, c],
            device_id=device,
            device_id_type=MESH,
        )

    def normalize(raw, half, inv, c):
        values = raw[window(c), :].astype(jnp.float32)
        scale = 1.0 / jnp.sqrt(jnp.sum(values * values, axis=-1, keepdims=True) + 1e-06)
        inv[window(c), :] = scale
        half[window(c), :] = (values * scale).astype(jnp.bfloat16)

    for load in loads:
        load.wait()
    for c in range(CHUNKS):
        normalize(txt_raw, txt_half, txt_inv, c)
        normalize(img_raw, img_half, img_inv, c)
        if c == 0:
            pl.semaphore_wait(barrier, greeted)
        remote(txt_half, mid_txt, 0, c, meet_next).start()
        remote(img_half, mid_img, 1, c, meet_prev).start()

    @pl.when(z != root)
    def _():
        signal(here_sem, at(x, y, jnp.where(z > root, z - 1, z + 1), core))

    @pl.when(base)
    def _():
        tell(0)

    def coefs(sims, diagonal):
        scaled = temp * sims
        logit = scaled + shift
        if not diagonal:
            return jax.nn.sigmoid(logit), scaled
        row = lax.broadcasted_iota(jnp.int32, sims.shape, 0)
        col = lax.broadcasted_iota(jnp.int32, sims.shape, 1)
        paired = row == col
        coef = jax.nn.sigmoid(jnp.where(paired, -logit, logit))
        return jnp.where(paired, -coef, coef), scaled

    coef, scaled = coefs(row_dot(img_half[...], txt_half[...]), True)
    own_c, own_cl = fold(coef), fold(coef * scaled)
    half = coef.astype(jnp.bfloat16)
    acc_img[...] = plain_dot(half, txt_half[...])
    half = coef.T.astype(jnp.bfloat16)
    acc_txt[...] = plain_dot(half, img_half[...])

    @pl.when(base)
    def _():
        pl.semaphore_wait(here_sem, root + min(1, z_n - 1 - root))
        for k in range(root):
            signal(base_sem, at(x, y, k, core))

    @pl.when(z != root)
    def _():
        pl.semaphore_wait(base_sem, 1)

    @pl.when(jnp.logical_and(z > root, z < z_n - 1))
    def _():
        pl.semaphore_wait(here_sem, 1)

    @pl.when(jnp.logical_and(z >= root, z < z_n - 1))
    def _():
        signal(base_sem, at(x, y, z + 1, core))

    def arrived(c):
        remote(txt_half, mid_txt, 0, c, meet_next).wait_recv()
        remote(img_half, mid_img, 1, c, meet_prev).wait_recv()

    def send_on(c):
        remote(mid_txt, end_txt, 2, c, second).start()
        remote(mid_img, end_img, 3, c, first).start()

    for c in range(CHUNKS):
        arrived(c)

    coef, scaled = coefs(row_dot(mid_img[...], mid_txt[...]), False)
    part[0:8, :] = own_c + fold(coef)
    part[8:16, :] = own_cl + fold(coef * scaled)
    tile = jnp.concatenate(
        [
            jnp.sum(part[0:8, :], axis=0, keepdims=True),
            jnp.sum(part[8:16, :], axis=0, keepdims=True),
            jnp.zeros((6, 128), jnp.float32),
        ],
        axis=0,
    )

    climb[slot] = tile

    def rise(k, place):
        return pltpu.make_async_remote_copy(
            src_ref=climb.at[place],
            dst_ref=climb.at[place],
            send_sem=rise_sem.at[k],
            recv_sem=climb_sem.at[place],
            device_id=rooted(k),
            device_id_type=MESH,
        )

    def drop(k):
        return pltpu.make_async_remote_copy(
            src_ref=total,
            dst_ref=total,
            send_sem=drop_sem.at[k],
            recv_sem=drop_sem.at[z_n],
            device_id=at(x, y, k, core),
            device_id_type=MESH,
        )

    @pl.when(z != root)
    def _():
        for k in range(CORES):
            rise(k, slot).start()
        for k in range(CORES):
            rise(k, slot).wait_send()

    @pl.when(base)
    def _():
        for k in range(1, CORES):
            rise(k, slot).start()
        for k in range(1, CORES):
            rise(k, slot).wait_send()

    for c in range(CHUNKS):
        send_on(c)

    @pl.when(base)
    def _():
        for turn in range(TURNS):
            pl.semaphore_wait(round_sem.at[turn], 4)
            if turn + 1 < TURNS:
                tell(turn + 1)

    def exchange(level, k):
        count, mine, place = levels[level]
        return pltpu.make_async_remote_copy(
            src_ref=sums.at[level, mine],
            dst_ref=sums.at[level, mine],
            send_sem=sum_send.at[level, k],
            recv_sem=sum_recv.at[level, mine],
            device_id=place(k),
            device_id_type=MESH,
        )

    def incoming(level, k):
        count, mine, place = levels[level]
        source = lax.rem(mine + k, count)
        return pltpu.make_async_remote_copy(
            src_ref=sums.at[level, source],
            dst_ref=sums.at[level, source],
            send_sem=sum_send.at[level, k],
            recv_sem=sum_recv.at[level, source],
            device_id=place(k),
            device_id_type=MESH,
        )

    def add_over(level, tile):
        count, mine, _ = levels[level]
        sums[level, mine] = tile
        for k in range(1, count):
            exchange(level, k).start()
        for k in range(1, count):
            incoming(level, k).wait_recv()
        tile = sums[level, 0]
        for k in range(1, count):
            tile = tile + sums[level, k]
        return tile

    def finish(raw, half, inv, acc, visitors, out):
        coef, _ = coefs(row_dot(half[...], visitors[...]), False)
        grad = temp * (acc[...] + plain_dot(coef.astype(jnp.bfloat16), visitors[...]))
        scale = inv[...]
        unit = raw[...].astype(jnp.float32) * scale
        inner = jnp.sum(unit * grad, axis=-1, keepdims=True)
        out[...] = (grad - unit * inner) * scale

    for c in range(CHUNKS):
        remote(mid_txt, end_txt, 2, c, second).wait_recv()
    finish(img_raw, img_half, img_inv, acc_img, end_txt, gi_out)
    for c in range(CHUNKS):
        remote(mid_img, end_img, 3, c, first).wait_recv()
    finish(txt_raw, txt_half, txt_inv, acc_txt, end_img, gt_out)

    others = [k for k in range(z_n) if k != root]

    @pl.when(base)
    def _():
        for k in others:
            for c in range(CORES):
                rise(0, k * CORES + c).wait_recv()
        for k in range(1, CORES):
            rise(k, root * CORES + lax.rem(core + k, CORES)).wait_recv()
        tile = climb[0]
        for k in range(1, z_n * CORES):
            tile = tile + climb[k]
        for level in range(len(levels)):
            tile = add_over(level, tile)
        total[...] = tile
        for k in others:
            drop(k).start()

    for c in range(CHUNKS):
        remote(txt_half, mid_txt, 0, c, meet_next).wait_send()
        remote(img_half, mid_img, 1, c, meet_prev).wait_send()
        remote(mid_txt, end_txt, 2, c, second).wait_send()
        remote(mid_img, end_img, 3, c, first).wait_send()

    @pl.when(z != root)
    def _():
        drop(z).wait_recv()

    @pl.when(base)
    def _():
        for level, (count, _, _) in enumerate(levels):
            for k in range(1, count):
                exchange(level, k).wait_send()
        for k in others:
            drop(k).wait_send()

    sum_out[...] = total[...]


def leave(pairs, gi_in, gt_in, sum_in, gi_out, gt_out, cl_out, c_out, sem):
    rows = gi_in.shape[0]
    step = rows // PARTS
    copies = []
    for c in range(PARTS):
        part = pl.ds(c * step, step)
        for k, (src, dst) in enumerate(((gi_in, gi_out), (gt_in, gt_out))):
            copies.append(
                pltpu.make_async_copy(src.at[part, :], dst.at[part, :], sem.at[k, c])
            )
    for copy in copies:
        copy.start()
    c_out[0] = jnp.sum(sum_in[0:1, :]) / pairs
    cl_out[0] = jnp.sum(sum_in[1:2, :]) / pairs
    for copy in copies:
        copy.wait()


def local(blk_n, grp_n, image, text, log_temp, bias):
    rows, width = image.shape
    z_n = grp_n // (Y_LO * CORES)
    most = max(blk_n // Y_HI, Y_HI * Y_LO, CORES)
    wide = jax.ShapeDtypeStruct((rows, width), jnp.float32)
    one = jax.ShapeDtypeStruct((1,), jnp.float32)
    slab = jax.ShapeDtypeStruct((8, 128), jnp.float32)
    half = pltpu.VMEM((rows, width), jnp.bfloat16)
    full = pltpu.VMEM((rows, width), jnp.float32)
    thin = pltpu.VMEM((rows, 1), jnp.float32)
    vmem = pl.BlockSpec(memory_space=pltpu.VMEM)
    smem = pl.BlockSpec(memory_space=pltpu.SMEM)
    hbm = pl.BlockSpec(memory_space=pltpu.HBM)
    dma, plain = pltpu.SemaphoreType.DMA, pltpu.SemaphoreType.REGULAR
    grads_and_sums = pl.pallas_call(
        functools.partial(kernel, (blk_n, grp_n)),
        out_shape=(wide, wide, slab),
        in_specs=[hbm, hbm, smem, smem],
        out_specs=(vmem, vmem, vmem),
        scratch_shapes=[
            half, half, half, half, thin, thin,
            half, half, half, half, full, full,
            pltpu.VMEM((2, most, 8, 128), jnp.float32),
            pltpu.VMEM((16, 128), jnp.float32),
            pltpu.VMEM((z_n * CORES, 8, 128), jnp.float32),
            pltpu.VMEM((8, 128), jnp.float32),
            dma((2,)), dma((4, CHUNKS)), dma((4, CHUNKS)),
            dma((2, most)), dma((2, most)), dma((CORES,)), dma((z_n * CORES,)), dma((z_n + 1,)),
            plain, plain, pltpu.SemaphoreType.REGULAR((TURNS,)),
        ],
        compiler_params=pltpu.CompilerParams(
            collective_id=0, has_side_effects=True, vmem_limit_bytes=40 << 20
        ),
        name="pair_gradients",
    )(
        pltpu.with_memory_space_constraint(image, pltpu.HBM),
        pltpu.with_memory_space_constraint(text, pltpu.HBM),
        log_temp,
        bias,
    )
    return pl.pallas_call(
        functools.partial(leave, float(rows * blk_n * grp_n)),
        out_shape=(wide, wide, one, one),
        in_specs=[vmem, vmem, vmem],
        out_specs=(hbm, hbm, smem, smem),
        scratch_shapes=[dma((2, PARTS))],
        compiler_params=pltpu.CompilerParams(vmem_limit_bytes=8 << 20),
        name="leave",
    )(*grads_and_sums)


def solution(mesh):
    rows = P(("blk", "grp"), None)
    return jax.shard_map(
        functools.partial(local, mesh.shape["blk"], mesh.shape["grp"]),
        mesh=mesh,
        in_specs=(rows, rows, P(), P()),
        out_specs=(rows, rows, P(), P()),
        check_vma=False,
    )
```

```python
import functools

import jax
import jax.numpy as jnp
from jax import lax
from jax.experimental import pallas as pl
from jax.experimental.pallas import tpu as pltpu
from jax.sharding import PartitionSpec as P

MESH = pl.DeviceIdType.MESH
Y_HI, Y_LO, CORES = 4, 2, 2
CHUNKS = 8
PARTS = 4
TURNS = 3


def row_dot(left, right):
    return lax.dot_general(
        left, right, (((1,), (1,)), ((), ())), preferred_element_type=jnp.float32
    )


def plain_dot(left, right):
    return lax.dot_general(
        left, right, (((1,), (0,)), ((), ())), preferred_element_type=jnp.float32
    )


def fold(tile):
    rows, cols = tile.shape
    part = jnp.sum(tile.reshape(rows // 8, 8, cols), axis=0)
    return functools.reduce(
        jnp.add, [part[:, at : at + 128] for at in range(0, cols, 128)]
    )


def kernel(
    sizes, img_in, txt_in, log_temp, bias, gi_out, gt_out, sum_out,
    img_raw, txt_raw, img_half, txt_half, img_inv, txt_inv,
    mid_txt, mid_img, end_txt, end_img, acc_txt, acc_img, sums,
    part, climb, total, load_sem, send_sem, recv_sem, sum_send, sum_recv, rise_sem, climb_sem, drop_sem,
    here_sem, base_sem, round_sem,
):
    blk_n, grp_n = sizes
    x_n, z_n = blk_n // Y_HI, grp_n // (Y_LO * CORES)
    rows = img_raw.shape[0]
    step = rows // CHUNKS

    me, grp = lax.axis_index("blk"), lax.axis_index("grp")
    x, y_hi = lax.div(me, Y_HI), lax.rem(me, Y_HI)
    z, low = lax.div(grp, Y_LO * CORES), lax.rem(grp, Y_LO * CORES)
    y_lo, core = lax.div(low, CORES), lax.rem(low, CORES)
    y = y_hi * Y_LO + y_lo

    def at(x, y, z, core):
        return (
            x * Y_HI + lax.div(y, Y_LO),
            z * (Y_LO * CORES) + lax.rem(y, Y_LO) * CORES + core,
        )

    other = z * (Y_LO * CORES) + (1 - y_lo) * CORES + core
    before = lax.rem(me + blk_n - 1, blk_n)
    meet_next = (x * Y_HI + lax.rem(y_hi + y_lo, Y_HI), other)
    meet_prev = (
        lax.div(before, Y_HI) * Y_HI + lax.rem(lax.rem(before, Y_HI) + y_lo, Y_HI),
        other,
    )
    first_blk = x * Y_HI + lax.rem(y_hi + y_lo + Y_HI - 1, Y_HI)
    first = (first_blk, other)
    second = (lax.rem(first_blk + 1, blk_n), other)

    root, chief = min(1, z_n - 1), CORES - 1
    base = z == root
    lead = jnp.logical_and(base, core == chief)
    slot, lead_slot = z * CORES + core, root * CORES + chief

    def along(k):
        return at(x, lax.rem(y + k, Y_HI * Y_LO), z, core)

    def across(k):
        return at(lax.rem(x + k, x_n), y, z, core)

    levels = (
        (Y_HI * Y_LO, y, along),
        (x_n, x, across),
    )

    loads = [
        pltpu.make_async_copy(img_in, img_raw, load_sem.at[0]),
        pltpu.make_async_copy(txt_in, txt_raw, load_sem.at[1]),
    ]
    for load in loads:
        load.start()

    barrier = pltpu.get_barrier_semaphore()

    def greet(device):
        pl.semaphore_signal(barrier, inc=1, device_id=device, device_id_type=MESH)

    for device in (meet_next, meet_prev, first, second):
        greet(device)

    @pl.when(jnp.logical_and(z >= root, z < z_n - 1))
    def _():
        greet(at(x, y, z + 1, core))

    beside = (across(1), across(x_n - 1), along(1), along(Y_HI * Y_LO - 1))

    @pl.when(lead)
    def _():
        greet(beside[0])
        greet(beside[1])

    @pl.when(base)
    def _():
        for k in range(1, CORES):
            greet(at(x, y, z, lax.rem(core + k, CORES)))
        for k in range(root):
            greet(at(x, y, k, core))

    greeted = 4 + jnp.where(base, CORES - 1, 1) + jnp.where(lead, 2, 0)

    def signal(sem, device):
        pl.semaphore_signal(sem, inc=1, device_id=device, device_id_type=MESH)

    def tell(turn):
        for device in beside:
            signal(round_sem.at[turn], device)

    temp = jnp.exp(jnp.full((1, 1), log_temp[0], jnp.float32))
    shift = bias[0]

    def window(c):
        return pl.ds(c * step, step)

    def remote(src, dst, kind, c, device):
        return pltpu.make_async_remote_copy(
            src_ref=src.at[window(c), :],
            dst_ref=dst.at[window(c), :],
            send_sem=send_sem.at[kind, c],
            recv_sem=recv_sem.at[kind, c],
            device_id=device,
            device_id_type=MESH,
        )

    def normalize(raw, half, inv, c):
        values = raw[window(c), :].astype(jnp.float32)
        scale = 1.0 / jnp.sqrt(jnp.sum(values * values, axis=-1, keepdims=True) + 1e-06)
        inv[window(c), :] = scale
        half[window(c), :] = (values * scale).astype(jnp.bfloat16)

    for load in loads:
        load.wait()
    for c in range(CHUNKS):
        normalize(txt_raw, txt_half, txt_inv, c)
        normalize(img_raw, img_half, img_inv, c)
        if c == 0:
            pl.semaphore_wait(barrier, greeted)
        remote(txt_half, mid_txt, 0, c, meet_next).start()
        remote(img_half, mid_img, 1, c, meet_prev).start()

    @pl.when(z != root)
    def _():
        signal(here_sem, at(x, y, jnp.where(z > root, z - 1, z + 1), core))

    @pl.when(lead)
    def _():
        tell(0)

    def coefs(sims, diagonal):
        scaled = temp * sims
        logit = scaled + shift
        if not diagonal:
            return jax.nn.sigmoid(logit), scaled
        row = lax.broadcasted_iota(jnp.int32, sims.shape, 0)
        col = lax.broadcasted_iota(jnp.int32, sims.shape, 1)
        paired = row == col
        coef = jax.nn.sigmoid(jnp.where(paired, -logit, logit))
        return jnp.where(paired, -coef, coef), scaled

    coef, scaled = coefs(row_dot(img_half[...], txt_half[...]), True)
    own_c, own_cl = fold(coef), fold(coef * scaled)
    half = coef.astype(jnp.bfloat16)
    acc_img[...] = plain_dot(half, txt_half[...])
    half = coef.T.astype(jnp.bfloat16)
    acc_txt[...] = plain_dot(half, img_half[...])

    @pl.when(base)
    def _():
        pl.semaphore_wait(here_sem, root + min(1, z_n - 1 - root))
        for k in range(root):
            signal(base_sem, at(x, y, k, core))

    @pl.when(z != root)
    def _():
        pl.semaphore_wait(base_sem, 1)

    @pl.when(jnp.logical_and(z > root, z < z_n - 1))
    def _():
        pl.semaphore_wait(here_sem, 1)

    @pl.when(jnp.logical_and(z >= root, z < z_n - 1))
    def _():
        signal(base_sem, at(x, y, z + 1, core))

    def arrived(c):
        remote(txt_half, mid_txt, 0, c, meet_next).wait_recv()
        remote(img_half, mid_img, 1, c, meet_prev).wait_recv()

    def send_on(c):
        remote(mid_txt, end_txt, 2, c, second).start()
        remote(mid_img, end_img, 3, c, first).start()

    for c in range(CHUNKS):
        arrived(c)

    coef, scaled = coefs(row_dot(mid_img[...], mid_txt[...]), False)
    part[0:8, :] = own_c + fold(coef)
    part[8:16, :] = own_cl + fold(coef * scaled)
    tile = jnp.concatenate(
        [
            jnp.sum(part[0:8, :], axis=0, keepdims=True),
            jnp.sum(part[8:16, :], axis=0, keepdims=True),
            jnp.zeros((6, 128), jnp.float32),
        ],
        axis=0,
    )

    climb[slot] = tile

    def rise(place):
        return pltpu.make_async_remote_copy(
            src_ref=climb.at[place],
            dst_ref=climb.at[place],
            send_sem=rise_sem,
            recv_sem=climb_sem.at[place],
            device_id=at(x, y, root, chief),
            device_id_type=MESH,
        )

    def drop(k):
        return pltpu.make_async_remote_copy(
            src_ref=total,
            dst_ref=total,
            send_sem=drop_sem.at[k],
            recv_sem=drop_sem.at[z_n * CORES],
            device_id=at(x, y, k // CORES, k % CORES),
            device_id_type=MESH,
        )

    follows = jnp.logical_not(lead)

    @pl.when(follows)
    def _():
        rise(slot).start()
        rise(slot).wait_send()

    for c in range(CHUNKS):
        send_on(c)

    @pl.when(lead)
    def _():
        for turn in range(TURNS):
            pl.semaphore_wait(round_sem.at[turn], 4)
            if turn + 1 < TURNS:
                tell(turn + 1)

    def exchange(level, k):
        count, mine, place = levels[level]
        return pltpu.make_async_remote_copy(
            src_ref=sums.at[level, mine],
            dst_ref=sums.at[level, mine],
            send_sem=sum_send.at[level, k],
            recv_sem=sum_recv.at[level, mine],
            device_id=place(k),
            device_id_type=MESH,
        )

    def incoming(level, k):
        count, mine, place = levels[level]
        source = lax.rem(mine + k, count)
        return pltpu.make_async_remote_copy(
            src_ref=sums.at[level, source],
            dst_ref=sums.at[level, source],
            send_sem=sum_send.at[level, k],
            recv_sem=sum_recv.at[level, source],
            device_id=place(k),
            device_id_type=MESH,
        )

    def add_over(level, tile):
        count, mine, _ = levels[level]
        sums[level, mine] = tile
        for k in range(1, count):
            exchange(level, k).start()
        for k in range(1, count):
            incoming(level, k).wait_recv()
        tile = sums[level, 0]
        for k in range(1, count):
            tile = tile + sums[level, k]
        return tile

    others = [k for k in range(z_n * CORES) if k != lead_slot]

    @pl.when(lead)
    def _():
        for k in others:
            rise(k).wait_recv()
        tile = climb[0]
        for k in range(1, z_n * CORES):
            tile = tile + climb[k]
        for level in range(len(levels)):
            tile = add_over(level, tile)
        total[...] = tile
        for k in others:
            drop(k).start()

    def finish(raw, half, inv, acc, visitors, out):
        coef, _ = coefs(row_dot(half[...], visitors[...]), False)
        grad = temp * (acc[...] + plain_dot(coef.astype(jnp.bfloat16), visitors[...]))
        scale = inv[...]
        unit = raw[...].astype(jnp.float32) * scale
        inner = jnp.sum(unit * grad, axis=-1, keepdims=True)
        out[...] = (grad - unit * inner) * scale

    for c in range(CHUNKS):
        remote(mid_txt, end_txt, 2, c, second).wait_recv()
    finish(img_raw, img_half, img_inv, acc_img, end_txt, gi_out)
    for c in range(CHUNKS):
        remote(mid_img, end_img, 3, c, first).wait_recv()
    finish(txt_raw, txt_half, txt_inv, acc_txt, end_img, gt_out)

    for c in range(CHUNKS):
        remote(txt_half, mid_txt, 0, c, meet_next).wait_send()
        remote(img_half, mid_img, 1, c, meet_prev).wait_send()
        remote(mid_txt, end_txt, 2, c, second).wait_send()
        remote(mid_img, end_img, 3, c, first).wait_send()

    @pl.when(follows)
    def _():
        drop(0).wait_recv()

    @pl.when(lead)
    def _():
        for level, (count, _, _) in enumerate(levels):
            for k in range(1, count):
                exchange(level, k).wait_send()
        for k in others:
            drop(k).wait_send()

    sum_out[...] = total[...]


def leave(pairs, gi_in, gt_in, sum_in, gi_out, gt_out, cl_out, c_out, sem):
    rows = gi_in.shape[0]
    step = rows // PARTS
    copies = []
    for c in range(PARTS):
        part = pl.ds(c * step, step)
        for k, (src, dst) in enumerate(((gi_in, gi_out), (gt_in, gt_out))):
            copies.append(
                pltpu.make_async_copy(src.at[part, :], dst.at[part, :], sem.at[k, c])
            )
    for copy in copies:
        copy.start()
    c_out[0] = jnp.sum(sum_in[0:1, :]) / pairs
    cl_out[0] = jnp.sum(sum_in[1:2, :]) / pairs
    for copy in copies:
        copy.wait()


def local(blk_n, grp_n, image, text, log_temp, bias):
    rows, width = image.shape
    z_n = grp_n // (Y_LO * CORES)
    most = max(blk_n // Y_HI, Y_HI * Y_LO, CORES)
    wide = jax.ShapeDtypeStruct((rows, width), jnp.float32)
    one = jax.ShapeDtypeStruct((1,), jnp.float32)
    slab = jax.ShapeDtypeStruct((8, 128), jnp.float32)
    half = pltpu.VMEM((rows, width), jnp.bfloat16)
    full = pltpu.VMEM((rows, width), jnp.float32)
    thin = pltpu.VMEM((rows, 1), jnp.float32)
    vmem = pl.BlockSpec(memory_space=pltpu.VMEM)
    smem = pl.BlockSpec(memory_space=pltpu.SMEM)
    hbm = pl.BlockSpec(memory_space=pltpu.HBM)
    dma, plain = pltpu.SemaphoreType.DMA, pltpu.SemaphoreType.REGULAR
    grads_and_sums = pl.pallas_call(
        functools.partial(kernel, (blk_n, grp_n)),
        out_shape=(wide, wide, slab),
        in_specs=[hbm, hbm, smem, smem],
        out_specs=(vmem, vmem, vmem),
        scratch_shapes=[
            half, half, half, half, thin, thin,
            half, half, half, half, full, full,
            pltpu.VMEM((2, most, 8, 128), jnp.float32),
            pltpu.VMEM((16, 128), jnp.float32),
            pltpu.VMEM((z_n * CORES, 8, 128), jnp.float32),
            pltpu.VMEM((8, 128), jnp.float32),
            dma((2,)), dma((4, CHUNKS)), dma((4, CHUNKS)),
            dma((2, most)), dma((2, most)), dma, dma((z_n * CORES,)), dma((z_n * CORES + 1,)),
            plain, plain, pltpu.SemaphoreType.REGULAR((TURNS,)),
        ],
        compiler_params=pltpu.CompilerParams(
            collective_id=0, has_side_effects=True, vmem_limit_bytes=40 << 20
        ),
        name="pair_gradients",
    )(
        pltpu.with_memory_space_constraint(image, pltpu.HBM),
        pltpu.with_memory_space_constraint(text, pltpu.HBM),
        log_temp,
        bias,
    )
    return pl.pallas_call(
        functools.partial(leave, float(rows * blk_n * grp_n)),
        out_shape=(wide, wide, one, one),
        in_specs=[vmem, vmem, vmem],
        out_specs=(hbm, hbm, smem, smem),
        scratch_shapes=[dma((2, PARTS))],
        compiler_params=pltpu.CompilerParams(vmem_limit_bytes=8 << 20),
        name="leave",
    )(*grads_and_sums)


def solution(mesh):
    rows = P(("blk", "grp"), None)
    return jax.shard_map(
        functools.partial(local, mesh.shape["blk"], mesh.shape["grp"]),
        mesh=mesh,
        in_specs=(rows, rows, P(), P()),
        out_specs=(rows, rows, P(), P()),
        check_vma=False,
    )
```
